32 devices in a mesh: dp: 4 (over z), mp: 8 (over y, x, core).
Axes of the slice: x: 2, y: 2, z: 4, core: 2. Of those that a mesh axis runs over, the one named last changes fastest.
Arguments:
- tokens_in: bfloat16 [2048, 3072], P(('dp', 'mp')), may hold values from -6 to 6
- out_grad: bfloat16 [2048, 3072], P(('dp', 'mp')), may hold values from -0.29882812 to 0.29882812
- w_up: bfloat16 [12288, 3072], P('mp'), may hold values from -0.109375 to 0.109375
- w_down: bfloat16 [12288, 3072], P('mp'), may hold values from -0.0546875 to 0.0546875
- mask_up: int32 [96, 24], P('mp'), may hold values 0 or 1
- mask_down: int32 [96, 24], P('mp'), may hold values 0 or 1
- order_up: int32 [48], replicated, may hold values from 0 to 47, each once
- order_down: int32 [48], replicated, may hold values from 0 to 47, each once
- moment_one: float32 [2, 8, 48, 32, 3072], P(None, 'mp', 'dp'), may hold values from -1.8 to 1.8
- moment_two: float32 [2, 8, 48, 32, 3072], P(None, 'mp', 'dp'), may hold values from 0.03 to 1
Outputs:
- input_grad: bfloat16 [2048, 3072], P(('dp', 'mp'))
- update_step: bfloat16 [2, 12288, 3072], P(None, 'mp')
The draws below stay inside these ranges and needn't reach their ends.
Inputs may be any that keep to these rules, and one draw needn't show every extreme that they name: `order_up`: each value of 0 to 47 appears once. `order_down`: each value of 0 to 47 appears once.
All inputs are finite; a program needn't handle non-finite values. No bound on the sum of `mask_up` or of `mask_down` on one device may be relied on, other than what follows from the above.
Results may differ from the reference program's by a relative error of at most 0.014.
Values may be sent and summed in bfloat16 or wider, within the bound.
A program may use at most 192 MiB of HBM per device.

```python
import math
import jax
import jax.numpy as jnp
from jax import lax

D = 3072
FFW = 12288
TOK_DEV = 64
BUCKET = 32
TOKENS = 2048
NBM = 48
OWNED = 12
N_DP = 4
N_MP = 8


def with_ends(array, key, low, largest):
    extent = array.shape
    spot = [jax.random.randint(jax.random.fold_in(key, axis), (), 0, extent[axis]) for axis in range(len(extent))]
    array = array.at[tuple(spot)].set(low)
    longest = extent.index(max(extent))
    spot[longest] = (spot[longest] + 1) % extent[longest]
    return array.at[tuple(spot)].set(largest)


def shard_levels(stream_key, extent, cuts, low, high):
    factor_of = 1.0
    for position, shards_of in cuts:
        draws = jax.random.uniform(jax.random.fold_in(jax.random.fold_in(stream_key, 6), position), (shards_of,), jnp.float32, low / len(cuts), high / len(cuts))
        factor_of = factor_of * jnp.repeat(jnp.exp(draws), extent[position] // shards_of).reshape((-1,) + (1,) * (len(extent) - 1 - position))
    return factor_of


def centred(stream_key, shape, spread, limit, shards=(), kind=jnp.bfloat16):
    array = jax.random.normal(stream_key, shape, jnp.float32) * spread
    if len(shards) > 0:
        array = shard_levels(stream_key, shape, shards, -0.22, 0.18) * array
    return jnp.clip(array, min=-limit, max=limit).astype(kind)


def setup_inputs(seed: int = 0) -> dict:
    key_of = jax.random.split(jax.random.key(seed), 11)
    return {
        "tokens_in": centred(key_of[0], (TOKENS, D), 1.0, 6.0, ((0, 32),)),
        "out_grad": centred(key_of[1], (TOKENS, D), 0.05, 0.29882812, ((0, 32),)),
        "w_up": centred(key_of[2], (FFW, D), D ** -0.5, 0.109375, ((0, 8),)),
        "w_down": centred(key_of[3], (FFW, D), FFW ** -0.5, 0.0546875, ((0, 8),)),
        "mask_up": with_ends((jax.random.randint(key_of[4], (FFW // 128, D // 128), 0, 2) < 1).astype(jnp.int32), jax.random.fold_in(key_of[4], 1), 0, 1),
        "mask_down": with_ends((jax.random.randint(key_of[5], (FFW // 128, D // 128), 0, 2) < 1).astype(jnp.int32), jax.random.fold_in(key_of[5], 1), 0, 1),
        "order_up": jax.random.permutation(key_of[6], NBM).astype(jnp.int32),
        "order_down": jax.random.permutation(key_of[7], NBM).astype(jnp.int32),
        "moment_one": centred(key_of[8], (2, N_MP, NBM, BUCKET, D), 0.3, 1.8, ((1, 8), (2, 4)), jnp.float32),
        "moment_two": jnp.clip(jnp.exp(math.log(1.0) - 3.506558 * jax.random.uniform(key_of[9], (2, N_MP, NBM, BUCKET, D), jnp.float32) ** shard_levels(key_of[9], (2, N_MP, NBM, BUCKET, D), ((1, 8), (2, 4)), -0.2, 0.2)), 0.03, 1.0),
    }


bias_first = 1.0 - 0.9 ** 10
bias_second = 1.0 - 0.95 ** 10

def expand_mask(blocks):
    block_rows, block_cols = blocks.shape
    wide = jnp.broadcast_to(blocks.astype(jnp.bfloat16)[:, None, :, None], (block_rows, 128, block_cols, 128))
    return wide.reshape(block_rows * 128, block_cols * 128)

def adam_step(summed, moment_a, moment_b, weight_rows, mask_rows):
    first_new = 0.9 * moment_a + 0.1 * summed
    second_new = 0.95 * moment_b + 0.05 * summed * summed
    update = first_new / bias_first / (jnp.sqrt(second_new / bias_second) + 1e-08)
    return (mask_rows * (update + 0.1 * weight_rows)).astype(jnp.bfloat16)

def owner_step(total, weight, keep, order_table, moment_one, moment_two, matrix):
    place = order_table % N_DP * OWNED + order_table // N_DP
    first_old = jnp.take(moment_one[matrix], place, axis=1)
    second_old = jnp.take(moment_two[matrix], place, axis=1)
    summed = total.reshape(N_MP, NBM, BUCKET, D)
    weight_rows = weight.astype(jnp.float32).reshape(N_MP, NBM, BUCKET, D)
    mask_rows = keep.astype(jnp.float32).reshape(N_MP, NBM, BUCKET, D)
    return adam_step(summed, first_old, second_old, weight_rows, mask_rows).reshape(FFW, D)

def reference(tokens_in, out_grad, w_up, w_down, mask_up, mask_down, order_up, order_down, moment_one, moment_two):
    keep_up = expand_mask(mask_up)
    keep_down = expand_mask(mask_down)
    up_live = w_up * keep_up
    down_live = w_down * keep_down
    group_rows = TOK_DEV * N_MP
    shard_width = FFW // N_MP
    grad_up = jnp.zeros((FFW, D), jnp.float32)
    grad_down = jnp.zeros((FFW, D), jnp.float32)
    input_parts = []
    for replica in range(N_DP):
        feat_rows = tokens_in[replica * group_rows:(replica + 1) * group_rows]
        grad_rows = out_grad[replica * group_rows:(replica + 1) * group_rows]
        hidden_pre = jnp.dot(feat_rows, up_live.T, preferred_element_type=jnp.float32)
        activation, gelu_back = jax.vjp(jax.nn.gelu, hidden_pre)
        act_low = activation.astype(jnp.bfloat16)
        part_down = (jnp.dot(act_low.T, grad_rows, preferred_element_type=jnp.float32) * keep_down).astype(jnp.bfloat16)
        act_grad = jnp.dot(grad_rows, down_live.T, preferred_element_type=jnp.float32)
        hidden_grad = gelu_back(act_grad)[0].astype(jnp.bfloat16)
        part_up = (jnp.dot(hidden_grad.T, feat_rows, preferred_element_type=jnp.float32) * keep_up).astype(jnp.bfloat16)
        grad_up = grad_up + lax.optimization_barrier(part_up).astype(jnp.float32)
        grad_down = grad_down + lax.optimization_barrier(part_down).astype(jnp.float32)
        input_total = jnp.zeros((group_rows, D), jnp.float32)
        for shard in range(N_MP):
            lo_unit = shard * shard_width
            partial_term = jnp.dot(hidden_grad[:, lo_unit:lo_unit + shard_width], up_live[lo_unit:lo_unit + shard_width], preferred_element_type=jnp.float32)
            input_total = input_total + lax.optimization_barrier(partial_term.astype(jnp.bfloat16)).astype(jnp.float32)
        input_parts.append(input_total.astype(jnp.bfloat16))
    step_up = owner_step(grad_up, w_up, keep_up, order_up, moment_one, moment_two, 0)
    step_down = owner_step(grad_down, w_down, keep_down, order_down, moment_one, moment_two, 1)
    return (jnp.concatenate(input_parts, axis=0), jnp.stack([step_up, step_down]))
```

```python
import functools

import jax
import jax.numpy as jnp
from jax import lax
from jax.experimental import pallas as pl
from jax.experimental.pallas import tpu as pltpu
from jax.sharding import PartitionSpec as P

MESH = pl.DeviceIdType.MESH
bias_first = 1.0 - 0.9**10
bias_second = 1.0 - 0.95**10


def gather_kernel(
    n_dp, n_mp, x_ref, g_ref, x_all, g_all, z_send, z_recv, r_send, r_recv, c_send, c_recv, l_sem
):
    d, m = lax.axis_index("dp"), lax.axis_index("mp")
    n = n_mp // 2
    q, core = m // 2, m % 2
    y, x = q // 2, q % 2
    spot = y + x * (n - 1 - 2 * y)

    def chip_at(p):
        far = p // (n // 2)
        return 2 * (p + far * (n - 1 - 2 * p)) + far

    sibling = q * 2 + 1 - core
    ahead = chip_at((spot + 1) % n) * 2 + core
    behind = chip_at((spot + n - 1) % n) * 2 + core
    offsets = [0]
    for k in range(1, n_dp):
        step = (k + 1) // 2
        offsets.append(step if k % 2 == 1 else n_dp - step)

    barrier = pltpu.get_barrier_semaphore()
    partners = [((d + k) % n_dp, m) for k in range(1, n_dp)]
    partners += [(d, ahead), (d, behind), (d, sibling)]
    for partner in partners:
        pl.semaphore_signal(barrier, inc=1, device_id=partner, device_id_type=MESH)
    pl.semaphore_wait(barrier, len(partners))

    own = (x_ref, g_ref)
    full = (x_all, g_all)
    turn = (1, n - 1)
    onward = (ahead, behind)

    def slot(arr, e, s, c):
        p = (spot + n - turn[arr] * s % n) % n
        return ((d + n_dp - offsets[e]) % n_dp) * n_mp + chip_at(p) * 2 + c

    def copy(src, dst, send, recv, device):
        return pltpu.make_async_remote_copy(
            src_ref=src,
            dst_ref=dst,
            send_sem=send,
            recv_sem=recv,
            device_id=device,
            device_id_type=MESH,
        )

    sends, locals_ = [], []

    def pass_on(arr, e, s):
        place = full[arr].at[slot(arr, e, s, core)]
        source = own[arr] if e == 0 and s == 0 else place
        if s < n - 1:
            sent = copy(
                source, place, r_send.at[arr, e, s], r_recv.at[arr, e, s + 1], (d, onward[arr])
            )
            sent.start()
            sends.append(sent)
        sent = copy(source, place, c_send.at[arr, e, s], c_recv.at[arr, e, s], (d, sibling))
        sent.start()
        sends.append(sent)

    for arr in range(2):
        pass_on(arr, 0, 0)
    for e in range(1, n_dp):
        for arr in range(2):
            sent = copy(
                own[arr],
                full[arr].at[d * n_mp + m],
                z_send.at[arr, e],
                z_recv.at[arr, e],
                ((d + offsets[e]) % n_dp, m),
            )
            sent.start()
            sends.append(sent)
    for arr in range(2):
        kept = pltpu.make_async_copy(own[arr], full[arr].at[d * n_mp + m], l_sem.at[arr])
        kept.start()
        locals_.append(kept)
    for wave in range(1, n_dp + n - 1):
        for e in range(n_dp):
            s = wave - e
            if s < 0 or s >= n:
                continue
            for arr in range(2):
                place = full[arr].at[slot(arr, e, s, core)]
                if s == 0:
                    copy(place, place, z_send.at[arr, e], z_recv.at[arr, e], (d, sibling)).wait_recv()
                else:
                    copy(
                        place, place, r_send.at[arr, e, s], r_recv.at[arr, e, s], (d, sibling)
                    ).wait_recv()
                pass_on(arr, e, s)
    for e in range(n_dp):
        for s in range(n):
            for arr in range(2):
                place = full[arr].at[slot(arr, e, s, 1 - core)]
                copy(
                    place, place, c_send.at[arr, e, s], c_recv.at[arr, e, s], (d, sibling)
                ).wait_recv()
    for sent in sends:
        sent.wait_send()
    for kept in locals_:
        kept.wait()


def gather_all(x, g, n_dp, n_mp):
    rows, width = x.shape
    n = n_mp // 2
    shape = jax.ShapeDtypeStruct((n_dp * n_mp, rows, width), x.dtype)
    any_spec = pl.BlockSpec(memory_space=pl.ANY)
    out = pl.pallas_call(
        functools.partial(gather_kernel, n_dp, n_mp),
        out_shape=(shape, shape),
        in_specs=[any_spec, any_spec],
        out_specs=(any_spec, any_spec),
        scratch_shapes=[
            pltpu.SemaphoreType.DMA((2, n_dp)),
            pltpu.SemaphoreType.DMA((2, n_dp)),
            pltpu.SemaphoreType.DMA((2, n_dp, n)),
            pltpu.SemaphoreType.DMA((2, n_dp, n)),
            pltpu.SemaphoreType.DMA((2, n_dp, n)),
            pltpu.SemaphoreType.DMA((2, n_dp, n)),
            pltpu.SemaphoreType.DMA((2,)),
        ],
        compiler_params=pltpu.CompilerParams(collective_id=0, has_side_effects=True),
        name="gather_tokens",
    )(x, g)
    return tuple(a.reshape(n_dp * n_mp * rows, width) for a in out)


def step_kernel(cols, owned, pos_ref, gu, gd, wu, wd, ma, mb, out):
    s, i = pl.program_id(0), pl.program_id(1)
    base = (s * owned + i) * cols

    def run(g_ref, w_ref):
        for c in range(cols):
            at = slice(c * 128, (c + 1) * 128)
            g = g_ref[0, :, at]
            first_new = 0.9 * ma[0, 0, 0, :, at] + 0.1 * g
            second_new = 0.95 * mb[0, 0, 0, :, at] + 0.05 * g * g
            update = first_new / bias_first / (jnp.sqrt(second_new / bias_second) + 1e-08)
            step = update + 0.1 * w_ref[0, :, at].astype(jnp.float32)
            out[pos_ref[base + c]] = step.astype(out.dtype)

    @pl.when(s == 0)
    def _():
        run(gu, wu)

    @pl.when(s == 1)
    def _():
        run(gd, wd)


def packed_steps(pos, gu, gd, wu, wd, moment_one, moment_two):
    owned, rows, width = gu.shape
    cols = width // 128
    moment = pl.BlockSpec((1, 1, 1, rows, width), lambda s, i, p: (s, 0, i, 0, 0))
    first = pl.BlockSpec((1, rows, width), lambda s, i, p: (i * (1 - s) + (owned - 1) * s, 0, 0))
    second = pl.BlockSpec((1, rows, width), lambda s, i, p: (i * s, 0, 0))
    tiles = 2 * owned * cols
    return pl.pallas_call(
        functools.partial(step_kernel, cols, owned),
        out_shape=jax.ShapeDtypeStruct((tiles, rows, 128), jnp.bfloat16),
        grid_spec=pltpu.PrefetchScalarGridSpec(
            num_scalar_prefetch=1,
            grid=(2, owned),
            in_specs=[first, second, first, second, moment, moment],
            out_specs=pl.BlockSpec((tiles, rows, 128), lambda s, i, p: (0, 0, 0)),
        ),
        compiler_params=pltpu.CompilerParams(vmem_limit_bytes=40 * 2**20),
        name="packed_steps",
    )(pos, gu, gd, wu, wd, moment_one, moment_two)


def spread_kernel(cols, per, table, packed, out):
    base = pl.program_id(0) * per * cols

    def bucket(k, carry):
        for c in range(cols):
            index = table[base + k * cols + c]
            at = slice(c * 128, (c + 1) * 128)

            @pl.when(index >= 0)
            def _():
                out[k, :, at] = packed[jnp.maximum(index, 0)]

            @pl.when(index < 0)
            def _():
                out[k, :, at] = jnp.zeros((out.shape[1], 128), out.dtype)

        return carry

    lax.fori_loop(0, per, bucket, 0)


def spread_steps(table, packed, total, cols):
    rows = packed.shape[1]
    per = 4
    return pl.pallas_call(
        functools.partial(spread_kernel, cols, per),
        out_shape=jax.ShapeDtypeStruct((total, rows, cols * 128), packed.dtype),
        grid_spec=pltpu.PrefetchScalarGridSpec(
            num_scalar_prefetch=1,
            grid=(total // per,),
            in_specs=[pl.BlockSpec(memory_space=pltpu.VMEM)],
            out_specs=pl.BlockSpec((per, rows, cols * 128), lambda i, t: (i, 0, 0)),
        ),
        compiler_params=pltpu.CompilerParams(vmem_limit_bytes=48 * 2**20),
        name="spread_steps",
    )(table, packed)


def shards(
    n_dp,
    n_mp,
    tokens_in,
    out_grad,
    w_up,
    w_down,
    mask_up,
    mask_down,
    order_up,
    order_down,
    moment_one,
    moment_two,
):
    hidden_local, width = w_up.shape
    buckets = order_up.shape[0]
    owned = buckets // n_dp
    bucket_rows = hidden_local // buckets
    cols = width // 128
    tiles = 2 * owned * cols
    owner_index = lax.axis_index("dp")
    row_of = jnp.arange(buckets) * bucket_rows // 128

    def by_owner(order):
        where = jnp.zeros((buckets,), jnp.int32).at[order].set(jnp.arange(buckets, dtype=jnp.int32))
        return where.reshape(owned, n_dp).T

    slots_up, slots_down = by_owner(order_up), by_owner(order_down)
    live = jnp.concatenate([mask_up[row_of[slots_up]], mask_down[row_of[slots_down]]], axis=1)
    live = live.reshape(n_dp, tiles)
    ahead = jnp.cumsum(live, axis=1)
    count = ahead[:, -1:]
    index = jnp.arange(tiles, dtype=jnp.int32)[None]
    pos = jnp.where(live > 0, ahead - 1, count + index - ahead).astype(jnp.int32)
    most = lax.pmax(jnp.max(count).astype(jnp.float32), "mp")
    pos_cube = pos.reshape(n_dp, 2, owned, cols)

    def live_part(weight, mask):
        blocks = weight.reshape(hidden_local // 128, 128, cols, 128)
        return (blocks * mask.astype(weight.dtype)[:, None, :, None]).reshape(hidden_local, width)

    up_live = live_part(w_up, mask_up)
    down_live = live_part(w_down, mask_down)
    mine_up, mine_down = slots_up[owner_index], slots_down[owner_index]

    def mm(a, b, dims):
        return lax.dot_general(a, b, (dims, ((), ())), preferred_element_type=jnp.float32)

    def rows_of(matrix, chosen):
        return matrix.reshape(buckets, bucket_rows, width)[chosen]

    gathered = n_dp * n_mp <= 64
    if gathered:
        x_all, g_all = gather_all(tokens_in, out_grad, n_dp, n_mp)
        group = x_all.shape[0] // n_dp
        x_rep = lax.dynamic_slice_in_dim(x_all, owner_index * group, group, 0)
        g_rep = lax.dynamic_slice_in_dim(g_all, owner_index * group, group, 0)
    else:
        x_rep = lax.all_gather(tokens_in, "mp", axis=0, tiled=True)
        g_rep = lax.all_gather(out_grad, "mp", axis=0, tiled=True)

    activation, gelu_back = jax.vjp(jax.nn.gelu, mm(x_rep, up_live, ((1,), (1,))))
    hidden_grad = gelu_back(mm(g_rep, down_live, ((1,), (1,))))[0].astype(jnp.bfloat16)
    partial_term = mm(hidden_grad, up_live, ((1,), (0,))).astype(jnp.bfloat16)
    if gathered:
        partial_term, x_all, g_all = lax.optimization_barrier((partial_term, x_all, g_all))
    input_grad = lax.psum_scatter(partial_term, "mp", scatter_dimension=0, tiled=True)

    if gathered:
        up_rows = rows_of(up_live, jnp.concatenate([mine_up, mine_down])).reshape(-1, width)
        down_rows = rows_of(down_live, mine_up).reshape(-1, width)
        half = owned * bucket_rows
        pre = mm(x_all, up_rows, ((1,), (1,)))
        act_low = jax.nn.gelu(pre[:, half:]).astype(jnp.bfloat16)
        _, owner_back = jax.vjp(jax.nn.gelu, pre[:, :half])
        grad_low = owner_back(mm(g_all, down_rows, ((1,), (1,))))[0].astype(jnp.bfloat16)
        grad_up = mm(grad_low, x_all, ((0,), (0,)))
        grad_down = mm(act_low, g_all, ((0,), (0,)))
    else:

        def to_owner(part, slots):
            by_slot = rows_of(part.astype(jnp.bfloat16), slots.reshape(-1))
            return lax.psum_scatter(by_slot, "dp", scatter_dimension=0, tiled=True)

        act_low = activation.astype(jnp.bfloat16)
        grad_up = to_owner(mm(hidden_grad, x_rep, ((0,), (0,))), slots_up).astype(jnp.float32)
        grad_down = to_owner(mm(act_low, g_rep, ((0,), (0,))), slots_down).astype(jnp.float32)
    packed = packed_steps(
        pos[owner_index],
        grad_up.reshape(owned, bucket_rows, width),
        grad_down.reshape(owned, bucket_rows, width),
        rows_of(w_up, mine_up),
        rows_of(w_down, mine_down),
        moment_one,
        moment_two,
    )

    def table_for(order, mask, matrix, size):
        owner, slot = order % n_dp, order // n_dp
        found = owner[:, None] * size + pos_cube[owner, matrix, slot]
        return jnp.where(mask[row_of] > 0, found, -1)

    def send(size, packed):
        table = jnp.concatenate(
            [table_for(order_up, mask_up, 0, size), table_for(order_down, mask_down, 1, size)]
        ).astype(jnp.int32)
        arrived = lax.all_gather(packed[:size], "dp", axis=0, tiled=True)
        return spread_steps(table.reshape(-1), arrived, 2 * buckets, cols)

    sizes = [-(-tiles * part // 12) for part in (6, 7, 8, 10, 12)]
    level = jnp.sum(most > jnp.asarray(sizes[:-1], jnp.float32)).astype(jnp.int32)
    steps = lax.switch(level, [functools.partial(send, size) for size in sizes], packed)
    return (input_grad, steps.reshape(2, hidden_local, width))


def solution(mesh):
    placed = (
        P(("dp", "mp"), None),
        P(("dp", "mp"), None),
        P("mp", None),
        P("mp", None),
        P("mp", None),
        P("mp", None),
        P(),
        P(),
        P(None, "mp", "dp", None, None),
        P(None, "mp", "dp", None, None),
    )
    return jax.shard_map(
        functools.partial(shards, mesh.shape["dp"], mesh.shape["mp"]),
        mesh=mesh,
        in_specs=placed,
        out_specs=(P(("dp", "mp"), None), P(None, "mp", None)),
        check_vma=False,
    )
```
